256 devices in a mesh: sparse: 8 (over y, x_lo), rows: 32 (over z, x_hi, core).
Axes of the slice: x: 4 (x_hi: 2, x_lo: 2; x = x_hi * 2 + x_lo), y: 4, z: 8, core: 2. Of those that a mesh axis runs over, the one named last changes fastest.
Arguments:
- env_desc: bfloat16 [262144, 2048], P(('sparse', 'rows')), may hold values from -0.29882812 to 1
- sparse_desc: bfloat16 [2048, 2048], P('sparse'), may hold values from -0.29882812 to 1
- extra_atoms: int32 [8, 1024], P('sparse'), may hold values from 1 to 64, 17408 in all within a row
- owner_slots: int32 [8, 1024], P('sparse'), may hold values from 0 to 31, as said below
Outputs:
- energy_rows: float32 [8192, 2048], P(('sparse', 'rows'))
The draws below stay inside these ranges and needn't reach their ends.
Inputs may be any that keep to these rules, and one draw needn't show every extreme that they name: Within each row of owner_slots, structures whose indices are equal modulo 32 have distinct values. The atoms of each row of extra_atoms fill exactly 1024 * 32 environments.
All inputs are finite; a program needn't handle non-finite values.
Results may differ from the reference program's by a relative error of at most 0.00087.
Values may be sent and summed in bfloat16 or wider, within the bound.
No kernel may reach another device: no remote copies, remote signals or barrier semaphores. Data moves between devices by JAX's collectives and lax.ppermute only.
A program may use at most 64 MiB of HBM per device.

```python
import math
import jax
import jax.numpy as jnp
import numpy as np
from jax import lax

W = 2048
ENV_DEV = 1024
STR_DEV = 32
ATOM_MIN = 16
SPG = 1024
NSTRUCT = 8192
M = 2048
NENV = 262144
N_SPARSE = 8
N_ROWS = 32


def draw_owner_slots(key, part):
    key = jax.random.fold_in(key, 7)
    keys = jax.random.split(key, N_SPARSE * N_ROWS)
    perms = jax.vmap(lambda one_key: jax.random.permutation(one_key, STR_DEV))(keys)
    perms = perms.reshape(N_SPARSE, N_ROWS, STR_DEV).transpose(0, 2, 1)
    return perms.reshape(N_SPARSE, STR_DEV * N_ROWS).astype(jnp.int32)


def block_levels(stream_key, extent, shards, smallest, high):
    level = 1.0
    for dim, parts in shards:
        draws = jax.random.uniform(jax.random.fold_in(jax.random.fold_in(stream_key, 6), dim), (parts,), jnp.float32, smallest / len(shards), high / len(shards))
        level = level * jnp.repeat(jnp.exp(draws), extent[dim] // parts).reshape((-1,) + (1,) * (len(extent) - 1 - dim))
    return level


def profile(count, total, limit, skew):
    portions = [(1 << 20) // math.isqrt(standing ** skew) + 1 for standing in range(2, count + 1)]
    rest, counts = total - limit - (count - 1), [1] * (count - 1)
    while rest > 0:
        movable = [i for i in range(count - 1) if counts[i] < limit]
        whole, remaining = sum([portions[i] for i in movable]), rest
        for i in movable:
            addition = min(limit - counts[i], max(1, remaining * portions[i] // whole), rest)
            counts[i] = counts[i] + addition
            rest = rest - addition
    return np.array([limit] + counts)


def uneven_parts(stream_key, number_of, total, bound, skew):
    if number_of == 2:
        one = jax.random.randint(stream_key, (), max(1, total - bound), min(bound, total - 1) + 1)
        return jnp.stack([one, total - one])
    tallies = jnp.asarray(profile(number_of, total, bound, skew), jnp.int32)
    pairs = (number_of - 1) // 2
    donor, sink = tallies[1:1 + 2 * pairs:2], tallies[2:2 + 2 * pairs:2]
    slack = jnp.minimum(donor - 1, bound - sink)
    shifted = jax.random.randint(jax.random.fold_in(stream_key, 1), (pairs,), 0, 1 << 20) % (slack + 1)
    tallies = tallies.at[1:1 + 2 * pairs:2].set(donor - shifted).at[2:2 + 2 * pairs:2].set(sink + shifted)
    return tallies[jax.random.permutation(jax.random.fold_in(stream_key, 2), number_of)]


def setup_inputs(seed: int = 0) -> dict:
    key_list = jax.random.split(jax.random.key(seed), 5)
    env_desc = jnp.clip(-0.29882812 + 1.2988281 * jax.random.uniform(key_list[0], (NENV, W), jnp.float32) ** block_levels(key_list[0], (NENV, W), ((0, 256),), -0.2, 0.2), -0.29882812, 1.0).astype(jnp.bfloat16)
    sparse_desc = jnp.clip(-0.29882812 + 1.2988281 * jax.random.uniform(key_list[1], (M, W), jnp.float32) ** block_levels(key_list[1], (M, W), ((0, 8),), -0.2, 0.2), -0.29882812, 1.0).astype(jnp.bfloat16)
    extra_atoms = jax.vmap(lambda own: uneven_parts(own, SPG, ENV_DEV * N_ROWS - SPG * (ATOM_MIN - 1), 4 * ATOM_MIN, 2))(jax.random.split(key_list[2], N_SPARSE)).reshape((N_SPARSE, SPG)).astype(jnp.int32)
    owner_slots = draw_owner_slots(jax.random.fold_in(key_list[4], 71), 0)
    return {"env_desc": env_desc, "sparse_desc": sparse_desc, "extra_atoms": extra_atoms, "owner_slots": owner_slots}


def unit_rows(desc):
    values = desc.astype(jnp.float32)
    return (values / jnp.sqrt(lax.optimization_barrier(jnp.sum(values * values, axis=1, keepdims=True)) + 1e-06)).astype(jnp.bfloat16)

def reference(env_desc, sparse_desc, extra_atoms, owner_slots):
    sparse_unit = unit_rows(sparse_desc)
    group_atoms = ENV_DEV * N_ROWS

    def one_group(index):
        rows_block = lax.dynamic_slice_in_dim(env_desc, (index * group_atoms).astype(jnp.int32), group_atoms, 0)
        env_unit = unit_rows(rows_block)
        inner = jnp.dot(env_unit, sparse_unit.T, preferred_element_type=jnp.float32)
        square = inner * inner
        kernel = square * square
        atoms = extra_atoms[index] + (ATOM_MIN - 1)
        ends = jnp.cumsum(atoms).astype(jnp.int32)
        position = jnp.arange(group_atoms, dtype=jnp.int32)
        owner = lax.optimization_barrier(jnp.sum((position[:, None] >= ends[None, :]).astype(jnp.int32), axis=1)).astype(jnp.int32)
        sums = jax.ops.segment_sum(kernel, owner, num_segments=SPG)
        energy = sums / atoms.astype(jnp.float32)[:, None]
        structure = jnp.arange(SPG, dtype=jnp.int32)
        target = (structure % N_ROWS * STR_DEV + owner_slots[index]).astype(jnp.int32)
        placed = jnp.zeros((SPG, M), jnp.float32).at[target].set(energy)
        return placed
    stacked = lax.map(one_group, jnp.arange(N_SPARSE, dtype=jnp.int32))
    return stacked.reshape(NSTRUCT, M)
```

```python
import jax
import jax.numpy as jnp
from jax import lax
from jax.experimental import pallas as pl
from jax.experimental.pallas import tpu as pltpu
from jax.sharding import PartitionSpec as P

Y, XL, Z, XH, CORE = 4, 2, 8, 2, 2
CHIPS = Z * XH
ROWS = CHIPS * CORE
HALO = 16
KEEP = 4
MIB = 1 << 20


def move(array, to):
    pairs = []
    for y in range(Y):
        for xl in range(XL):
            for z in range(Z):
                for xh in range(XH):
                    for core in range(CORE):
                        target = to(y, xl, z, xh, core)
                        if target is not None:
                            pairs.append((place(y, xl, z, xh, core), place(*target)))
    return lax.ppermute(array, ("sparse", "rows"), pairs)


def place(y, xl, z, xh, core):
    return (((y % Y * XL + xl) * Z + z % Z) * XH + xh) * CORE + core


def up(y, xl, z, xh, core):
    return y + 1, xl, z, xh, core


def down(y, xl, z, xh, core):
    return y - 1, xl, z, xh, core


def across(y, xl, z, xh, core):
    return y, 1 - xl, z, xh, core


def around(y, xl, z, xh, core):
    return y, 1 - xl, z, (xh + 1) % XH, core


def other_core(y, xl, z, xh, core):
    return y, xl, z, xh, 1 - core


def next_chip(to_core):
    def to(y, xl, z, xh, core):
        if core == 0:
            return None
        return y, xl, (z if xh == 0 else z + 1), 1 - xh, to_core

    return to


def unit(desc):
    values = desc.astype(jnp.float32)
    scale = 1.0 / jnp.sqrt(jnp.sum(values * values, axis=1, keepdims=True) + 1e-06)
    return (values * scale).astype(jnp.bfloat16)


def sparse_unit_kernel(core_ref, desc_ref, a_ref, b_ref):
    quarter = a_ref.shape[0]
    at = pl.multiple_of(core_ref[0] * (2 * quarter), 2 * quarter)
    a_ref[...] = unit(desc_ref[pl.ds(at, quarter), :])
    b_ref[...] = unit(desc_ref[pl.ds(at + quarter, quarter), :])


def sparse_unit(core, desc):
    rows, width = desc.shape
    piece = jax.ShapeDtypeStruct((rows // 4, width), jnp.bfloat16)
    return pl.pallas_call(
        sparse_unit_kernel,
        in_specs=[
            pl.BlockSpec(memory_space=pltpu.SMEM),
            pl.BlockSpec(memory_space=pltpu.VMEM),
        ],
        out_specs=[pl.BlockSpec(memory_space=pltpu.VMEM)] * 2,
        out_shape=[piece, piece],
        compiler_params=pltpu.CompilerParams(vmem_limit_bytes=16 * MIB),
        cost_estimate=pl.CostEstimate(
            flops=4 * rows * width, bytes_accessed=4 * rows * width, transcendentals=rows
        ),
    )(core, desc)


def env_unit_kernel(desc_ref, out_ref):
    out_ref[...] = unit(desc_ref[...])


def env_unit(desc):
    rows, width = desc.shape
    tile = 128
    return pl.pallas_call(
        env_unit_kernel,
        grid=(rows // tile,),
        in_specs=[pl.BlockSpec((tile, width), lambda i: (i, 0))],
        out_specs=pl.BlockSpec((tile, width), lambda i: (i, 0)),
        out_shape=jax.ShapeDtypeStruct((rows, width), jnp.bfloat16),
        compiler_params=pltpu.CompilerParams(vmem_limit_bytes=16 * MIB),
        cost_estimate=pl.CostEstimate(
            flops=6 * rows * width, bytes_accessed=4 * rows * width, transcendentals=rows
        ),
    )(desc)


def power_sums(env, block, member):
    inner = lax.dot_general(env, block, (((1,), (1,)), ((), ())), preferred_element_type=jnp.float32)
    square = inner * inner
    kernel = square * square
    high = kernel.astype(jnp.bfloat16)
    low = (kernel - high.astype(jnp.float32)).astype(jnp.bfloat16)
    return jnp.dot(member, high, preferred_element_type=jnp.float32) + jnp.dot(
        member, low, preferred_element_type=jnp.float32
    )


def main_kernel(
    p0, p1, p2, p3, own, other, halo, of_own, of_other, of_halo, out_ref, block, total
):
    step = pl.program_id(0)

    @pl.when(step == 0)
    def _():
        quarter = p0.shape[0]
        for i, piece in enumerate((p0, p1, p2, p3)):
            block[i * quarter : (i + 1) * quarter, :] = piece[...]
        total[...] = power_sums(unit(halo[...]), block[...], of_halo[...])

    total[...] += power_sums(own[...], block[...], of_own[...])
    total[...] += power_sums(other[...], block[...], of_other[...])

    @pl.when(step == pl.num_programs(0) - 1)
    def _():
        sums = total[...].reshape(ROWS // 2, 2 * KEEP, 256)
        left, right = sums[:, :, :128], sums[:, :, 128:]
        lower = lax.broadcasted_iota(jnp.int32, left.shape, 1) < KEEP
        out_ref[:, 0] = jnp.where(lower, left, jnp.roll(right, KEEP, axis=1))
        out_ref[:, 1] = jnp.where(lower, jnp.roll(left, KEEP, axis=1), right)


def main(pieces, own, other, halo, members):
    rows, width = own.shape
    tile = 256
    quarter = pieces[0].shape[0]
    columns = 4 * quarter
    of_own, of_other, of_halo = members
    count = of_own.shape[0]
    whole = lambda i: (0, 0)
    return pl.pallas_call(
        main_kernel,
        grid=(rows // tile,),
        in_specs=[pl.BlockSpec((quarter, width), whole)] * 4
        + [pl.BlockSpec((tile, width), lambda i: (i, 0))] * 2
        + [pl.BlockSpec((HALO, width), whole)]
        + [pl.BlockSpec((count, tile), lambda i: (0, i))] * 2
        + [pl.BlockSpec((count, HALO), whole)],
        out_specs=pl.BlockSpec((ROWS // 2, 2, 2 * KEEP, 128), lambda i: (0, 0, 0, 0)),
        out_shape=jax.ShapeDtypeStruct((ROWS // 2, 2, 2 * KEEP, 128), jnp.float32),
        scratch_shapes=[
            pltpu.VMEM((columns, width), jnp.bfloat16),
            pltpu.VMEM((count, columns), jnp.float32),
        ],
        compiler_params=pltpu.CompilerParams(vmem_limit_bytes=32 * MIB),
        cost_estimate=pl.CostEstimate(
            flops=4 * rows * width * columns, bytes_accessed=4 * rows * width, transcendentals=0
        ),
    )(*pieces, own, other, halo, of_own, of_other, of_halo)


def combine_kernel(column_ref, got_ref, pick_ref, atoms_ref, out_ref):
    pick = pick_ref[...]
    count = pick.shape[0] // 2
    for core in range(CORE):
        for call in range(4):
            rows = got_ref[:, core, 8 * call : 8 * (call + 1), :].reshape(8 * CHIPS, 128)
            high = rows.astype(jnp.bfloat16)
            rest = rows - high.astype(jnp.float32)
            mid = rest.astype(jnp.bfloat16)
            low = (rest - mid.astype(jnp.float32)).astype(jnp.bfloat16)
            sums = (
                jnp.dot(pick, low, preferred_element_type=jnp.float32)
                + jnp.dot(pick, mid, preferred_element_type=jnp.float32)
                + jnp.dot(pick, high, preferred_element_type=jnp.float32)
            )
            for half in range(2):
                at = pl.multiple_of(column_ref[(core * 4 + call) * 2 + half] * 128, 128)
                out_ref[:, pl.ds(at, 128)] = sums[half * count : (half + 1) * count] / atoms_ref[...]


def combine(columns, got, pick, atoms, width):
    count = pick.shape[0] // 2
    return pl.pallas_call(
        combine_kernel,
        in_specs=[pl.BlockSpec(memory_space=pltpu.SMEM)]
        + [pl.BlockSpec(memory_space=pltpu.VMEM)] * 3,
        out_specs=pl.BlockSpec(memory_space=pltpu.VMEM),
        out_shape=jax.ShapeDtypeStruct((count, width), jnp.float32),
        compiler_params=pltpu.CompilerParams(vmem_limit_bytes=16 * MIB),
    )(columns, got, pick, atoms)


def on_device(env_desc, sparse_desc, extra_atoms, owner_slots):
    env_rows, _ = env_desc.shape
    block_cols = sparse_desc.shape[0]
    groups = extra_atoms.shape[1]
    str_dev = groups // ROWS
    atom_min = env_rows // (2 * str_dev)
    my_block, my_row = lax.axis_index("sparse"), lax.axis_index("rows")
    y, xl = my_block // XL, my_block % XL
    chip, core = my_row // CORE, my_row % CORE

    a, b = sparse_unit(core.reshape(1).astype(jnp.int32), sparse_desc)
    up_a, down_b = move(a, up), move(b, down)
    near_a, near_b = move(a, across), move(b, around)
    up_b, down_a = move(b, up), move(a, down)
    own = env_unit(env_desc)
    tail = env_desc[env_rows - HALO :]
    halo = jnp.where(core == 0, move(tail, next_chip(0)), move(tail, next_chip(1)))
    other = move(own, other_core)
    far_a, far_b = move(up_a, up), move(down_b, down)
    near_up_a, near_down_b = move(up_a, across), move(down_b, around)
    near_up_b, near_down_a = move(up_b, around), move(down_a, across)
    near_far_a, near_far_b = move(far_a, across), move(far_b, around)

    atoms = extra_atoms[0] + (atom_min - 1)
    slots = owner_slots[0]
    ends = jnp.cumsum(atoms)
    starts = ends - atoms
    chip_rows = CORE * env_rows
    bases = jnp.arange(CHIPS, dtype=jnp.int32) * chip_rows
    firsts = jnp.sum((ends[None, :] <= bases[:, None]).astype(jnp.int32), axis=1)
    chips = jnp.arange(CHIPS, dtype=jnp.int32)
    first = jnp.sum(jnp.where(chips == chip, firsts, 0))
    before = jnp.sum(jnp.where(chips == chip - 1, firsts, 0))
    base = chip * chip_rows
    spilled = (chip > 0) & (first - before == ROWS * KEEP)
    owners = jnp.arange(ROWS, dtype=jnp.int32)[:, None]
    keeps = jnp.arange(KEEP, dtype=jnp.int32)[None, :]
    held = (first + (owners - first) % ROWS + ROWS * keeps).reshape(-1)
    structure = jnp.arange(groups, dtype=jnp.int32)
    select = (structure[None, :] == held[:, None]).astype(jnp.int32)
    held_start = jnp.sum(select * starts[None, :], axis=1)
    held_end = jnp.sum(select * ends[None, :], axis=1)
    lower = jnp.maximum(held_start, jnp.where(spilled, base - HALO, base))[:, None]
    upper = held_end[:, None]

    def member(begin, count):
        position = begin + jnp.arange(count, dtype=jnp.int32)[None, :]
        return ((position >= lower) & (position < upper)).astype(jnp.bfloat16)

    members = (
        member(base + core * env_rows, env_rows),
        member(base + (1 - core) * env_rows, env_rows),
        member(base - HALO, HALO),
    )

    sent = firsts[:, None] + (my_row - firsts[:, None]) % ROWS + ROWS * keeps
    select = (structure[None, :] == sent.reshape(-1)[:, None]).astype(jnp.int32)
    slot = jnp.sum(select * (slots[None, :] + 1), axis=1).reshape(1, 1, CHIPS, 1, KEEP) - 1
    rows = jnp.arange(str_dev, dtype=jnp.int32).reshape(1, str_dev, 1, 1, 1)
    half = jnp.arange(2, dtype=jnp.int32)
    same = half.reshape(2, 1, 1, 1, 1) == half.reshape(1, 1, 1, 2, 1)
    pick = ((slot == rows) & same).astype(jnp.bfloat16).reshape(2 * str_dev, CHIPS * 2 * KEEP)
    mine = structure % ROWS == my_row
    owned = jnp.arange(str_dev, dtype=jnp.int32)
    match = ((slots[None, :] == owned[:, None]) & mine[None, :]).astype(jnp.int32)
    owned_atoms = jnp.sum(match * atoms[None, :], axis=1).astype(jnp.float32)[:, None]
    shifts = jnp.array([[0, 0], [0, 1], [3, 0], [1, 0], [3, 1], [1, 1], [2, 0], [2, 1]], jnp.int32)
    blocks = (y + shifts[:, 0]) % Y * XL + (xl + shifts[:, 1]) % XL
    columns = (blocks[None, :] * 2 + jnp.arange(CORE, dtype=jnp.int32)[:, None]).reshape(-1)

    sums = [
        main(pieces, own, other, halo, members)
        for pieces in (
            (a, b, near_a, near_b),
            (up_a, up_b, down_a, down_b),
            (near_up_a, near_up_b, near_down_a, near_down_b),
            (far_a, far_b, near_far_a, near_far_b),
        )
    ]
    partial_sums = jnp.concatenate(sums, axis=2).reshape(ROWS, 8 * 4, 128)
    got = lax.all_to_all(partial_sums, "rows", 0, 0, tiled=True)
    return combine(
        columns.astype(jnp.int32),
        got.reshape(CHIPS, CORE, 8 * 4, 128),
        pick,
        owned_atoms,
        block_cols * Y * XL,
    )


def solution(mesh):
    placed = (P(("sparse", "rows"), None), P("sparse", None), P("sparse", None), P("sparse", None))
    return jax.shard_map(
        on_device,
        mesh=mesh,
        in_specs=placed,
        out_specs=P(("sparse", "rows"), None),
        check_vma=False,
    )
```

```python
import functools

import jax
import jax.numpy as jnp
from jax import lax
from jax.experimental import pallas as pl
from jax.experimental.pallas import tpu as pltpu
from jax.sharding import PartitionSpec as P

Y, XL, Z, XH, CORE = 4, 2, 8, 2, 2
CHIPS = Z * XH
ROWS = CHIPS * CORE
KEEP = 4
HELD = ROWS * KEEP
HELD_ROWS = HELD + 8
SENT = 8 * KEEP + 8
LANES = 128
MIB = 1 << 20
SHIFTS = ((0, 0), (0, 1), (3, 0), (1, 0), (3, 1), (1, 1), (2, 0), (2, 1))
STEPS, LEAST, ZERO = 512.0, 126.0, 32768

VMEM = pl.BlockSpec(memory_space=pltpu.VMEM)
ANY = pl.BlockSpec(memory_space=pl.ANY)


def place(y, xl, z, xh, core):
    return (((y % Y * XL + xl) * Z + z % Z) * XH + xh) * CORE + core


def move(array, to):
    pairs = []
    for y in range(Y):
        for xl in range(XL):
            for z in range(Z):
                for xh in range(XH):
                    for core in range(CORE):
                        target = to(y, xl, z, xh, core)
                        if target is not None:
                            pairs.append((place(y, xl, z, xh, core), place(*target)))
    return lax.ppermute(array, ("sparse", "rows"), pairs)


def up(y, xl, z, xh, core):
    return y + 1, xl, z, xh, core


def down(y, xl, z, xh, core):
    return y - 1, xl, z, xh, core


def across(y, xl, z, xh, core):
    return y, 1 - xl, z, (xh + core) % XH, core


def onward(y, xl, z, xh, core):
    return (y + 1 if core == 0 else y - 1), xl, z, xh, core


def other_core(y, xl, z, xh, core):
    return y, xl, z, xh, 1 - core


def unit(desc):
    values = desc.astype(jnp.float32)
    scale = 1.0 / jnp.sqrt(jnp.sum(values * values, axis=1, keepdims=True) + 1e-06)
    return (values * scale).astype(jnp.bfloat16)


def in_hbm(array):
    return pltpu.with_memory_space_constraint(array, pltpu.HBM)


def in_vmem(array):
    return pltpu.with_memory_space_constraint(array, pltpu.VMEM)


def params(mib):
    return pltpu.CompilerParams(vmem_limit_bytes=mib * MIB)


def cost(flops, moved):
    return pl.CostEstimate(flops=flops, bytes_accessed=moved, transcendentals=0)


def sparse_kernel(desc_ref, half_ref, raw, sem):
    half = half_ref.shape[0]
    at = pl.multiple_of(lax.axis_index("rows") % CORE * half, half)
    copy = pltpu.make_async_copy(desc_ref.at[pl.ds(at, half)], raw, sem)
    copy.start()
    copy.wait()
    half_ref[...] = unit(raw[...])


def sparse_unit(desc):
    rows, width = desc.shape
    half = rows // CORE
    return pl.pallas_call(
        sparse_kernel,
        in_specs=[ANY],
        out_specs=VMEM,
        out_shape=jax.ShapeDtypeStruct((half, width), jnp.bfloat16),
        scratch_shapes=[pltpu.VMEM((half, width), jnp.bfloat16), pltpu.SemaphoreType.DMA],
        compiler_params=params(8),
        cost_estimate=cost(4 * half * width, 4 * half * width),
        name="sparse_unit",
    )(in_hbm(desc))


def env_kernel(own_desc, other_desc, *refs):
    own_ref, other_ref, raw, sems = refs[-4:]
    rows = own_desc.shape[0]
    tiles = sems.shape[0] // 2
    tile = rows // tiles
    steps = []
    for env, (desc, out) in enumerate(((own_desc, own_ref), (other_desc, other_ref))):
        for i in range(tiles):
            copy = pltpu.make_async_copy(
                desc.at[pl.ds(i * tile, tile)],
                raw.at[env, pl.ds(i * tile, tile)],
                sems.at[env * tiles + i],
            )
            steps.append((copy, env, out, slice(i * tile, (i + 1) * tile)))
    for copy, *_ in steps:
        copy.start()
    for copy, env, out, to in steps:
        copy.wait()
        out[to] = unit(raw[env, to])


def env_unit(own, other, after):
    rows, width = own.shape
    whole = jax.ShapeDtypeStruct((rows, width), jnp.bfloat16)
    return pl.pallas_call(
        env_kernel,
        in_specs=[ANY] * (2 + len(after)),
        out_specs=[VMEM] * 2,
        out_shape=[whole, whole],
        scratch_shapes=[
            pltpu.VMEM((CORE, rows, width), jnp.bfloat16),
            pltpu.SemaphoreType.DMA((8,)),
        ],
        compiler_params=params(24),
        cost_estimate=cost(16 * rows * width, 8 * rows * width),
        name="env_unit",
    )(in_hbm(own), other, *after)


def choose_kernel(up_ref, down_ref, *refs):
    first = lax.axis_index("rows") % CORE == 0
    refs[-1][...] = jnp.where(first, up_ref[...], down_ref[...])


def choose(from_up, from_down, after):
    return pl.pallas_call(
        choose_kernel,
        in_specs=[VMEM, VMEM] + [ANY] * len(after),
        out_specs=VMEM,
        out_shape=jax.ShapeDtypeStruct(from_up.shape, from_up.dtype),
        compiler_params=params(4),
        cost_estimate=cost(0, 6 * from_up.size),
        name="choose",
    )(from_up, from_down, *after)


def hold_kernel(array_ref, *refs):
    refs[-1][...] = array_ref[...]


def hold(array, after):
    return pl.pallas_call(
        hold_kernel,
        in_specs=[VMEM] + [ANY] * len(after),
        out_specs=VMEM,
        out_shape=jax.ShapeDtypeStruct(array.shape, array.dtype),
        compiler_params=params(4),
        cost_estimate=cost(0, 4 * array.size),
        name="hold",
    )(array, *after)


def book_kernel(
    extra_ref,
    slots_ref,
    own_ref,
    other_ref,
    inverse_ref,
    more_owner_ref,
    pick_ref,
    pick_more_ref,
    *,
    env_rows,
):
    groups = extra_ref.shape[1]
    parts = groups // LANES
    atom_min = env_rows // (2 * (groups // ROWS))
    chip_rows = CORE * env_rows
    my_row = lax.axis_index("rows")
    core = my_row % CORE
    chip = my_row // CORE
    base = chip * chip_rows

    def rows_of(ref):
        return jnp.concatenate([ref[:, i * LANES : (i + 1) * LANES] for i in range(parts)], axis=0)

    atoms = rows_of(extra_ref) + (atom_min - 1)
    slots = rows_of(slots_ref)
    lane_i = lax.broadcasted_iota(jnp.int32, (LANES, LANES), 0)
    lane_j = lax.broadcasted_iota(jnp.int32, (LANES, LANES), 1)
    upto = (lane_i <= lane_j).astype(jnp.float32)
    along = jnp.dot(
        atoms.astype(jnp.float32).astype(jnp.bfloat16),
        upto.astype(jnp.bfloat16),
        preferred_element_type=jnp.float32,
    )
    rows_total = along[:, LANES - 1 :].astype(jnp.int32)
    ends = along.astype(jnp.int32)
    part = lax.broadcasted_iota(jnp.int32, (parts, LANES), 0)
    for i in range(parts - 1):
        ends = ends + jnp.where(part > i, rows_total[i : i + 1, :], 0)
    starts = ends - atoms

    found = (ends <= base).astype(jnp.int32)
    first = jnp.sum(jnp.sum(found, axis=0, keepdims=True), axis=1, keepdims=True)

    row = lax.broadcasted_iota(jnp.int32, (HELD_ROWS, 1), 0)
    held = first + ((row // KEEP - first) & (ROWS - 1)) + ROWS * (row % KEEP)
    held = jnp.where(row < HELD, held, jnp.where(row == HELD, first + HELD, -1))
    more_owner_ref[...] = jnp.broadcast_to((first + HELD) & (ROWS - 1), more_owner_ref.shape)
    lane = lax.broadcasted_iota(jnp.int32, (HELD_ROWS, LANES), 1)
    found_start = jnp.zeros((HELD_ROWS, LANES), jnp.int32)
    found_end = jnp.zeros((HELD_ROWS, LANES), jnp.int32)
    for i in range(parts):
        here = held == lane + i * LANES
        found_start = jnp.where(here, starts[i : i + 1, :], found_start)
        found_end = jnp.where(here, ends[i : i + 1, :], found_end)
    start = jnp.sum(found_start, axis=1, keepdims=True)
    end = jnp.sum(found_end, axis=1, keepdims=True)
    inverse_ref[...] = 1.0 / jnp.maximum(end - start, 1).astype(jnp.float32)
    lower = jnp.maximum(start, base)

    def member(begin, count):
        position = begin + lax.broadcasted_iota(jnp.int32, (HELD_ROWS, count), 1)
        inside = (position >= lower) & (position < end)
        return inside.astype(jnp.float32).astype(jnp.bfloat16)

    own_ref[...] = member(base + core * env_rows, env_rows)
    other_ref[...] = member(base + (1 - core) * env_rows, env_rows)

    ends_down = ends.astype(jnp.float32).T.astype(jnp.int32)
    slots_down = slots.astype(jnp.float32).T.astype(jnp.int32)
    from_lane = lax.broadcasted_iota(jnp.int32, (1, LANES), 1)
    limit = (from_lane // (2 * KEEP)) * chip_rows
    ended = jnp.zeros((LANES, LANES), jnp.int32)
    for i in range(parts):
        ended = ended + (ends_down[:, i : i + 1] <= limit).astype(jnp.int32)
    firsts = jnp.sum(ended, axis=0, keepdims=True)
    sent = firsts + ((my_row - firsts) & (ROWS - 1)) + ROWS * (from_lane % KEEP)
    below = lax.broadcasted_iota(jnp.int32, (LANES, LANES), 0)
    more = firsts + HELD

    def slot_of(structure):
        found = jnp.zeros((LANES, LANES), jnp.int32)
        for i in range(parts):
            found = jnp.where(structure == below + i * LANES, slots_down[:, i : i + 1] + 1, found)
        return jnp.sum(found, axis=0, keepdims=True) - 1

    def picks(ref, slot, part):
        count = groups // ROWS
        target = lax.broadcasted_iota(jnp.int32, ref.shape, 0)
        chosen = (target % count == slot) & (target // count == part)
        ref[...] = chosen.astype(jnp.float32).astype(jnp.bfloat16)

    picks(pick_ref, slot_of(sent), (from_lane // KEEP) % 2)
    more_slot = jnp.where((more & (ROWS - 1)) == my_row, slot_of(more), -1)
    picks(pick_more_ref, more_slot, from_lane % 8)


def book(extra_atoms, owner_slots, env_rows):
    str_dev = extra_atoms.shape[1] // ROWS

    return pl.pallas_call(
        functools.partial(book_kernel, env_rows=env_rows),
        in_specs=[VMEM, VMEM],
        out_specs=[VMEM] * 6,
        out_shape=[
            jax.ShapeDtypeStruct((HELD_ROWS, env_rows), jnp.bfloat16),
            jax.ShapeDtypeStruct((HELD_ROWS, env_rows), jnp.bfloat16),
            jax.ShapeDtypeStruct((HELD_ROWS, 1), jnp.float32),
            jax.ShapeDtypeStruct((1, LANES), jnp.int32),
            jax.ShapeDtypeStruct((2 * str_dev, LANES), jnp.bfloat16),
            jax.ShapeDtypeStruct((8 * str_dev, LANES), jnp.bfloat16),
        ],
        compiler_params=params(8),
        cost_estimate=cost(1 << 22, 1 << 20),
        name="book",
    )(extra_atoms, owner_slots)


def power_parts(env, block):
    inner = lax.dot_general(env, block, (((1,), (1,)), ((), ())), preferred_element_type=jnp.float32)
    square = inner * inner
    kernel = square * square
    high = kernel.astype(jnp.bfloat16)
    return high, (kernel - high.astype(jnp.float32)).astype(jnp.bfloat16)


def block_sums(a, b, own, other, of_own, of_other, block, high, low):
    half = a.shape[0]
    block[:half] = a[...]
    block[half:] = b[...]
    rows = own.shape[0]
    tile = 512
    for begin, env in ((0, own), (rows, other)):
        for i in range(0, rows, tile):
            to = slice(begin + i, begin + i + tile)
            high[to], low[to] = power_parts(env[i : i + tile], block[...])

    def dot(member, part):
        return jnp.dot(member[...], part, preferred_element_type=jnp.float32)

    return (
        dot(of_own, high[:rows])
        + dot(of_own, low[:rows])
        + dot(of_other, high[rows:])
        + dot(of_other, low[rows:])
    )


def early_call(a, b, own, other, of_own, of_other, out, block, high, low):
    out[...] = block_sums(a, b, own, other, of_own, of_other, block, high, low)


def encode(sums):
    position = (jnp.log2(jnp.maximum(sums, 1e-37)) + LEAST) * STEPS
    code = jnp.clip(jnp.round(position), 0.0, 65534.0).astype(jnp.int32) + (1 - ZERO)
    return jnp.where(sums >= 2.0**-126, code, -ZERO)


def decode(codes):
    code = codes.astype(jnp.int32) + (ZERO - 1)
    return jnp.where(code < 0, 0.0, jnp.exp2(code.astype(jnp.float32) * (1.0 / STEPS) - LEAST))


def last_call(sums_0, sums_1, sums_2, inverse, more_owner, *refs):
    *operands, out_ref, block, high, low = refs
    last = block_sums(*operands, block, high, low)
    means = [part * inverse[...] for part in (sums_0[...], sums_1[...], sums_2[...], last)]
    tiles = (ROWS // 2, 2 * KEEP, LANES)
    lower = lax.broadcasted_iota(jnp.int32, tiles, 1) < KEEP
    owner = 2 * lax.broadcasted_iota(jnp.int32, tiles, 0)
    packed = ([], [])
    more = []
    for mean in means:
        both = encode(mean[:HELD]).reshape(ROWS // 2, 2 * KEEP, 2 * LANES)
        left, right = both[:, :, :LANES], both[:, :, LANES:]
        packed[0].append(jnp.where(lower, left, jnp.roll(right, KEEP, axis=1)))
        packed[1].append(jnp.where(lower, jnp.roll(left, KEEP, axis=1), right))
        more += [mean[HELD : HELD + 1, :LANES], mean[HELD : HELD + 1, LANES:]]
    codes = encode(jnp.concatenate(more, axis=0)).reshape(1, 8, LANES)
    for i in range(2):
        here = owner + i == more_owner[...].reshape(1, 1, LANES)
        packed[i].append(jnp.where(here, codes, -ZERO))
    rows = packed[0] + packed[1]
    for i in range(0, len(rows), 2):
        both = jnp.concatenate(rows[i : i + 2], axis=1)
        out_ref[:, 8 * i : 8 * i + 16] = both.astype(jnp.int16)


def call(kernel, first, pieces, envs, members, out_shape):
    own, other = envs
    rows, width = own.shape
    columns = 2 * LANES
    operands = (*first, *pieces, in_vmem(own), in_vmem(other), *members)
    return pl.pallas_call(
        kernel,
        in_specs=[VMEM] * len(operands),
        out_specs=VMEM,
        out_shape=out_shape,
        scratch_shapes=[
            pltpu.VMEM((columns, width), jnp.bfloat16),
            pltpu.VMEM((2 * rows, columns), jnp.bfloat16),
            pltpu.VMEM((2 * rows, columns), jnp.bfloat16),
        ],
        compiler_params=params(16),
        cost_estimate=cost(4 * rows * width * columns, 4 * rows * width),
        name=kernel.__name__,
    )(*operands)


def combine_kernel(got_ref, pick_ref, pick_more_ref, out_ref):
    block = lax.axis_index("sparse")
    y, xl = block // XL, block % XL
    count = out_ref.shape[0]
    tiles = []
    for i in range(CORE * SENT // 16):
        values = decode(got_ref[:, 16 * i : 16 * (i + 1), :])
        for j in range(2):
            tiles.append(values[:, 8 * j : 8 * (j + 1), :].reshape(8 * CHIPS, LANES))

    def picked(pick, tile):
        high = tile.astype(jnp.bfloat16)
        low = (tile - high.astype(jnp.float32)).astype(jnp.bfloat16)
        return jnp.dot(pick, high, preferred_element_type=jnp.float32) + jnp.dot(
            pick, low, preferred_element_type=jnp.float32
        )

    for core in range(CORE):
        *held, more = tiles[core * SENT // 8 : (core + 1) * SENT // 8]
        more = picked(pick_more_ref[...], more)
        for i, tile in enumerate(held):
            sums = picked(pick_ref[...], tile) + more[2 * i * count : 2 * (i + 1) * count]
            for half in range(2):
                dy, dx = SHIFTS[2 * i + half]
                column = ((y + dy) % Y * XL + (xl + dx) % XL) * CORE + core
                at = pl.multiple_of(column * LANES, LANES)
                out_ref[:, pl.ds(at, LANES)] = sums[half * count : (half + 1) * count]


def combine(got, pick, pick_more, width):
    return pl.pallas_call(
        combine_kernel,
        in_specs=[VMEM, VMEM, VMEM],
        out_specs=VMEM,
        out_shape=jax.ShapeDtypeStruct((pick.shape[0] // 2, width), jnp.float32),
        compiler_params=params(8),
        name="combine",
    )(got, pick, pick_more)


def on_device(env_desc, sparse_desc, extra_atoms, owner_slots):
    env_rows, _ = env_desc.shape
    width = sparse_desc.shape[0] * Y * XL
    other_desc = move(env_desc, other_core)
    half = sparse_unit(sparse_desc)
    from_up, from_down = move(half, up), move(half, down)
    near = move(half, across)
    *members, inverse, more_owner, pick, pick_more = book(extra_atoms, owner_slots, env_rows)
    envs = env_unit(env_desc, other_desc, (near, inverse))
    sums = jax.ShapeDtypeStruct((HELD_ROWS, 2 * LANES), jnp.float32)
    sums_0 = call(early_call, (), (half, near), envs, members, sums)
    far = move(choose(from_up, from_down, (sums_0,)), onward)
    near_up, near_down = move(from_up, across), move(from_down, across)
    sums_1 = call(early_call, (), (from_up, from_down), envs, members, sums)
    near_far = move(hold(far, (sums_1,)), across)
    sums_2 = call(early_call, (), (near_up, near_down), envs, members, sums)
    codes = call(
        last_call,
        (sums_0, sums_1, sums_2, inverse, more_owner),
        (far, near_far),
        envs,
        members,
        jax.ShapeDtypeStruct((ROWS // 2, 2 * SENT, LANES), jnp.int16),
    )
    got = lax.all_to_all(codes.reshape(ROWS, SENT, LANES), "rows", 0, 0, tiled=True)
    return combine(got.reshape(CHIPS, CORE * SENT, LANES), pick, pick_more, width)


def solution(mesh):
    placed = (P(("sparse", "rows"), None), P("sparse", None), P("sparse", None), P("sparse", None))
    return jax.shard_map(
        on_device,
        mesh=mesh,
        in_specs=placed,
        out_specs=P(("sparse", "rows"), None),
        check_vma=False,
    )
```

```python
import functools

import jax
import jax.numpy as jnp
from jax import lax
from jax.experimental import pallas as pl
from jax.experimental.pallas import tpu as pltpu
from jax.sharding import PartitionSpec as P

Y, XL, Z, XH, CORE = 4, 2, 8, 2, 2
CHIPS = Z * XH
ROWS = CHIPS * CORE
KEEP = 4
HELD = ROWS * KEEP
HELD_ROWS = HELD + 8
SENT = 8 * KEEP + 8
LANES = 128
MIB = 1 << 20
SHIFTS = ((0, 0), (0, 1), (3, 0), (1, 0), (3, 1), (1, 1), (2, 0), (2, 1))
STEPS, LEAST, ZERO = 512.0, 126.0, 32768

VMEM = pl.BlockSpec(memory_space=pltpu.VMEM)
ANY = pl.BlockSpec(memory_space=pl.ANY)


def place(y, xl, z, xh, core):
    return (((y % Y * XL + xl) * Z + z % Z) * XH + xh) * CORE + core


def move(array, to):
    pairs = []
    for y in range(Y):
        for xl in range(XL):
            for z in range(Z):
                for xh in range(XH):
                    for core in range(CORE):
                        target = to(y, xl, z, xh, core)
                        if target is not None:
                            pairs.append((place(y, xl, z, xh, core), place(*target)))
    return lax.ppermute(array, ("sparse", "rows"), pairs)


def up(y, xl, z, xh, core):
    return y + 1, xl, z, xh, core


def down(y, xl, z, xh, core):
    return y - 1, xl, z, xh, core


def across(y, xl, z, xh, core):
    return y, 1 - xl, z, (xh + core) % XH, core


def onward(y, xl, z, xh, core):
    return (y + 1 if core == 0 else y - 1), xl, z, xh, core


def opposite(y, xl, z, xh, core):
    return y + 2, xl, z, xh, core


def other_core(y, xl, z, xh, core):
    return y, xl, z, xh, 1 - core


def unit(desc):
    values = desc.astype(jnp.float32)
    scale = 1.0 / jnp.sqrt(jnp.sum(values * values, axis=1, keepdims=True) + 1e-06)
    return (values * scale).astype(jnp.bfloat16)


def in_hbm(array):
    return pltpu.with_memory_space_constraint(array, pltpu.HBM)


def in_vmem(array):
    return pltpu.with_memory_space_constraint(array, pltpu.VMEM)


def params(mib):
    return pltpu.CompilerParams(vmem_limit_bytes=mib * MIB)


def cost(flops, moved):
    return pl.CostEstimate(flops=flops, bytes_accessed=moved, transcendentals=0)


def sparse_kernel(desc_ref, half_ref, raw, sem):
    half = half_ref.shape[0]
    at = pl.multiple_of(lax.axis_index("rows") % CORE * half, half)
    copy = pltpu.make_async_copy(desc_ref.at[pl.ds(at, half)], raw, sem)
    copy.start()
    copy.wait()
    half_ref[...] = unit(raw[...])


def sparse_unit(desc):
    rows, width = desc.shape
    half = rows // CORE
    return pl.pallas_call(
        sparse_kernel,
        in_specs=[ANY],
        out_specs=VMEM,
        out_shape=jax.ShapeDtypeStruct((half, width), jnp.bfloat16),
        scratch_shapes=[pltpu.VMEM((half, width), jnp.bfloat16), pltpu.SemaphoreType.DMA],
        compiler_params=params(8),
        cost_estimate=cost(4 * half * width, 4 * half * width),
        name="sparse_unit",
    )(in_hbm(desc))


def env_kernel(own_desc, other_desc, *refs):
    own_ref, other_ref, raw, sems = refs[-4:]
    rows = own_desc.shape[0]
    tiles = sems.shape[0] // 2
    tile = rows // tiles
    steps = []
    for env, (desc, out) in enumerate(((own_desc, own_ref), (other_desc, other_ref))):
        for i in range(tiles):
            copy = pltpu.make_async_copy(
                desc.at[pl.ds(i * tile, tile)],
                raw.at[env, pl.ds(i * tile, tile)],
                sems.at[env * tiles + i],
            )
            steps.append((copy, env, out, slice(i * tile, (i + 1) * tile)))
    for copy, *_ in steps:
        copy.start()
    for copy, env, out, to in steps:
        copy.wait()
        out[to] = unit(raw[env, to])


def env_unit(own, other, after):
    rows, width = own.shape
    whole = jax.ShapeDtypeStruct((rows, width), jnp.bfloat16)
    return pl.pallas_call(
        env_kernel,
        in_specs=[ANY] * (2 + len(after)),
        out_specs=[VMEM] * 2,
        out_shape=[whole, whole],
        scratch_shapes=[
            pltpu.VMEM((CORE, rows, width), jnp.bfloat16),
            pltpu.SemaphoreType.DMA((8,)),
        ],
        compiler_params=params(24),
        cost_estimate=cost(16 * rows * width, 8 * rows * width),
        name="env_unit",
    )(in_hbm(own), other, *after)


def choose_kernel(up_ref, down_ref, *refs):
    first = lax.axis_index("rows") % CORE == 0
    refs[-1][...] = jnp.where(first, up_ref[...], down_ref[...])


def choose(from_up, from_down, after):
    return pl.pallas_call(
        choose_kernel,
        in_specs=[VMEM, VMEM] + [ANY] * len(after),
        out_specs=VMEM,
        out_shape=jax.ShapeDtypeStruct(from_up.shape, from_up.dtype),
        compiler_params=params(4),
        cost_estimate=cost(0, 6 * from_up.size),
        name="choose",
    )(from_up, from_down, *after)


def rows_kernel(array_ref, *refs, begin):
    refs[-1][...] = array_ref[begin : begin + refs[-1].shape[0]]


def rows_of(array, begin, count, after):
    width = array.shape[1]
    return pl.pallas_call(
        functools.partial(rows_kernel, begin=begin),
        in_specs=[VMEM] + [ANY] * len(after),
        out_specs=VMEM,
        out_shape=jax.ShapeDtypeStruct((count, width), array.dtype),
        compiler_params=params(4),
        cost_estimate=cost(0, 4 * count * width),
        name="rows_of",
    )(array, *after)


def book_kernel(
    extra_ref,
    slots_ref,
    own_ref,
    other_ref,
    inverse_ref,
    more_owner_ref,
    pick_ref,
    pick_more_ref,
    *,
    env_rows,
):
    groups = extra_ref.shape[1]
    parts = groups // LANES
    atom_min = env_rows // (2 * (groups // ROWS))
    chip_rows = CORE * env_rows
    my_row = lax.axis_index("rows")
    core = my_row % CORE
    chip = my_row // CORE
    base = chip * chip_rows

    def rows_of(ref):
        return jnp.concatenate([ref[:, i * LANES : (i + 1) * LANES] for i in range(parts)], axis=0)

    atoms = rows_of(extra_ref) + (atom_min - 1)
    slots = rows_of(slots_ref)
    lane_i = lax.broadcasted_iota(jnp.int32, (LANES, LANES), 0)
    lane_j = lax.broadcasted_iota(jnp.int32, (LANES, LANES), 1)
    upto = (lane_i <= lane_j).astype(jnp.float32)
    along = jnp.dot(
        atoms.astype(jnp.float32).astype(jnp.bfloat16),
        upto.astype(jnp.bfloat16),
        preferred_element_type=jnp.float32,
    )
    rows_total = along[:, LANES - 1 :].astype(jnp.int32)
    ends = along.astype(jnp.int32)
    part = lax.broadcasted_iota(jnp.int32, (parts, LANES), 0)
    for i in range(parts - 1):
        ends = ends + jnp.where(part > i, rows_total[i : i + 1, :], 0)
    starts = ends - atoms

    found = (ends <= base).astype(jnp.int32)
    first = jnp.sum(jnp.sum(found, axis=0, keepdims=True), axis=1, keepdims=True)

    row = lax.broadcasted_iota(jnp.int32, (HELD_ROWS, 1), 0)
    held = first + ((row // KEEP - first) & (ROWS - 1)) + ROWS * (row % KEEP)
    held = jnp.where(row < HELD, held, jnp.where(row == HELD, first + HELD, -1))
    more_owner_ref[...] = jnp.broadcast_to((first + HELD) & (ROWS - 1), more_owner_ref.shape)
    lane = lax.broadcasted_iota(jnp.int32, (HELD_ROWS, LANES), 1)
    found_start = jnp.zeros((HELD_ROWS, LANES), jnp.int32)
    found_end = jnp.zeros((HELD_ROWS, LANES), jnp.int32)
    for i in range(parts):
        here = held == lane + i * LANES
        found_start = jnp.where(here, starts[i : i + 1, :], found_start)
        found_end = jnp.where(here, ends[i : i + 1, :], found_end)
    start = jnp.sum(found_start, axis=1, keepdims=True)
    end = jnp.sum(found_end, axis=1, keepdims=True)
    inverse_ref[...] = 1.0 / jnp.maximum(end - start, 1).astype(jnp.float32)
    lower = jnp.maximum(start, base)

    def member(begin, count):
        position = begin + lax.broadcasted_iota(jnp.int32, (HELD_ROWS, count), 1)
        inside = (position >= lower) & (position < end)
        return inside.astype(jnp.float32).astype(jnp.bfloat16)

    own_ref[...] = member(base + core * env_rows, env_rows)
    other_ref[...] = member(base + (1 - core) * env_rows, env_rows)

    ends_down = ends.astype(jnp.float32).T.astype(jnp.int32)
    slots_down = slots.astype(jnp.float32).T.astype(jnp.int32)
    from_lane = lax.broadcasted_iota(jnp.int32, (1, LANES), 1)
    limit = (from_lane // (2 * KEEP)) * chip_rows
    ended = jnp.zeros((LANES, LANES), jnp.int32)
    for i in range(parts):
        ended = ended + (ends_down[:, i : i + 1] <= limit).astype(jnp.int32)
    firsts = jnp.sum(ended, axis=0, keepdims=True)
    sent = firsts + ((my_row - firsts) & (ROWS - 1)) + ROWS * (from_lane % KEEP)
    below = lax.broadcasted_iota(jnp.int32, (LANES, LANES), 0)
    more = firsts + HELD

    def slot_of(structure):
        found = jnp.zeros((LANES, LANES), jnp.int32)
        for i in range(parts):
            found = jnp.where(structure == below + i * LANES, slots_down[:, i : i + 1] + 1, found)
        return jnp.sum(found, axis=0, keepdims=True) - 1

    def picks(ref, slot, part):
        count = groups // ROWS
        target = lax.broadcasted_iota(jnp.int32, ref.shape, 0)
        chosen = (target % count == slot) & (target // count == part)
        ref[...] = chosen.astype(jnp.float32).astype(jnp.bfloat16)

    picks(pick_ref, slot_of(sent), (from_lane // KEEP) % 2)
    more_slot = jnp.where((more & (ROWS - 1)) == my_row, slot_of(more), -1)
    picks(pick_more_ref, more_slot, from_lane % 8)


def book(extra_atoms, owner_slots, env_rows):
    str_dev = extra_atoms.shape[1] // ROWS

    return pl.pallas_call(
        functools.partial(book_kernel, env_rows=env_rows),
        in_specs=[VMEM, VMEM],
        out_specs=[VMEM] * 6,
        out_shape=[
            jax.ShapeDtypeStruct((HELD_ROWS, env_rows), jnp.bfloat16),
            jax.ShapeDtypeStruct((HELD_ROWS, env_rows), jnp.bfloat16),
            jax.ShapeDtypeStruct((HELD_ROWS, 1), jnp.float32),
            jax.ShapeDtypeStruct((1, LANES), jnp.int32),
            jax.ShapeDtypeStruct((2 * str_dev, LANES), jnp.bfloat16),
            jax.ShapeDtypeStruct((8 * str_dev, LANES), jnp.bfloat16),
        ],
        compiler_params=params(8),
        cost_estimate=cost(1 << 22, 1 << 20),
        name="book",
    )(extra_atoms, owner_slots)


def power_parts(env, block):
    inner = lax.dot_general(env, block, (((1,), (1,)), ((), ())), preferred_element_type=jnp.float32)
    square = inner * inner
    kernel = square * square
    high = kernel.astype(jnp.bfloat16)
    return high, (kernel - high.astype(jnp.float32)).astype(jnp.bfloat16)


def block_sums(*refs):
    *pieces, own, other, of_own, of_other, block, high, low = refs
    at = 0
    for piece in pieces:
        block[at : at + piece.shape[0]] = piece[...]
        at += piece.shape[0]
    rows = own.shape[0]
    tile = 512
    for begin, env in ((0, own), (rows, other)):
        for i in range(0, rows, tile):
            to = slice(begin + i, begin + i + tile)
            high[to], low[to] = power_parts(env[i : i + tile], block[...])

    def dot(member, part):
        return jnp.dot(member[...], part, preferred_element_type=jnp.float32)

    return (
        dot(of_own, high[:rows])
        + dot(of_own, low[:rows])
        + dot(of_other, high[rows:])
        + dot(of_other, low[rows:])
    )


def early_call(a, b, own, other, of_own, of_other, out, block, high, low):
    out[...] = block_sums(a, b, own, other, of_own, of_other, block, high, low)


def encode(sums):
    position = (jnp.log2(jnp.maximum(sums, 1e-37)) + LEAST) * STEPS
    code = jnp.clip(jnp.round(position), 0.0, 65534.0).astype(jnp.int32) + (1 - ZERO)
    return jnp.where(sums >= 2.0**-126, code, -ZERO)


def decode(codes):
    code = codes.astype(jnp.int32) + (ZERO - 1)
    return jnp.where(code < 0, 0.0, jnp.exp2(code.astype(jnp.float32) * (1.0 / STEPS) - LEAST))


def last_call(sums_0, sums_1, sums_2, inverse, more_owner, *refs):
    *operands, out_ref, block, high, low = refs
    last = block_sums(*operands, block, high, low)
    near = jnp.concatenate([sums_2[:, :LANES], last[:, :LANES]], axis=1)
    far = jnp.concatenate([sums_2[:, LANES:], last[:, LANES:]], axis=1)
    means = [part * inverse[...] for part in (sums_0[...], sums_1[...], near, far)]
    tiles = (ROWS // 2, 2 * KEEP, LANES)
    lower = lax.broadcasted_iota(jnp.int32, tiles, 1) < KEEP
    owner = 2 * lax.broadcasted_iota(jnp.int32, tiles, 0)
    packed = ([], [])
    more = []
    for mean in means:
        both = encode(mean[:HELD]).reshape(ROWS // 2, 2 * KEEP, 2 * LANES)
        left, right = both[:, :, :LANES], both[:, :, LANES:]
        packed[0].append(jnp.where(lower, left, jnp.roll(right, KEEP, axis=1)))
        packed[1].append(jnp.where(lower, jnp.roll(left, KEEP, axis=1), right))
        more += [mean[HELD : HELD + 1, :LANES], mean[HELD : HELD + 1, LANES:]]
    codes = encode(jnp.concatenate(more, axis=0)).reshape(1, 8, LANES)
    for i in range(2):
        here = owner + i == more_owner[...].reshape(1, 1, LANES)
        packed[i].append(jnp.where(here, codes, -ZERO))
    rows = packed[0] + packed[1]
    for i in range(0, len(rows), 2):
        both = jnp.concatenate(rows[i : i + 2], axis=1)
        out_ref[:, 8 * i : 8 * i + 16] = both.astype(jnp.int16)


def call(kernel, first, pieces, envs, members, out_shape):
    own, other = envs
    rows, width = own.shape
    columns = 2 * LANES
    operands = (*first, *pieces, in_vmem(own), in_vmem(other), *members)
    return pl.pallas_call(
        kernel,
        in_specs=[VMEM] * len(operands),
        out_specs=VMEM,
        out_shape=out_shape,
        scratch_shapes=[
            pltpu.VMEM((columns, width), jnp.bfloat16),
            pltpu.VMEM((2 * rows, columns), jnp.bfloat16),
            pltpu.VMEM((2 * rows, columns), jnp.bfloat16),
        ],
        compiler_params=params(16),
        cost_estimate=cost(4 * rows * width * columns, 4 * rows * width),
        name=kernel.__name__,
    )(*operands)


def combine_kernel(got_ref, pick_ref, pick_more_ref, out_ref):
    block = lax.axis_index("sparse")
    y, xl = block // XL, block % XL
    count = out_ref.shape[0]
    tiles = []
    for i in range(CORE * SENT // 16):
        values = decode(got_ref[:, 16 * i : 16 * (i + 1), :])
        for j in range(2):
            tiles.append(values[:, 8 * j : 8 * (j + 1), :].reshape(8 * CHIPS, LANES))

    def picked(pick, tile):
        high = tile.astype(jnp.bfloat16)
        low = (tile - high.astype(jnp.float32)).astype(jnp.bfloat16)
        return jnp.dot(pick, high, preferred_element_type=jnp.float32) + jnp.dot(
            pick, low, preferred_element_type=jnp.float32
        )

    for core in range(CORE):
        *held, more = tiles[core * SENT // 8 : (core + 1) * SENT // 8]
        more = picked(pick_more_ref[...], more)
        for i, tile in enumerate(held):
            sums = picked(pick_ref[...], tile) + more[2 * i * count : 2 * (i + 1) * count]
            for half in range(2):
                dy, dx = SHIFTS[2 * i + half]
                column = ((y + dy) % Y * XL + (xl + dx) % XL) * CORE + core
                at = pl.multiple_of(column * LANES, LANES)
                out_ref[:, pl.ds(at, LANES)] = sums[half * count : (half + 1) * count]


def combine(got, pick, pick_more, width):
    return pl.pallas_call(
        combine_kernel,
        in_specs=[VMEM, VMEM, VMEM],
        out_specs=VMEM,
        out_shape=jax.ShapeDtypeStruct((pick.shape[0] // 2, width), jnp.float32),
        compiler_params=params(8),
        name="combine",
    )(got, pick, pick_more)


def on_device(env_desc, sparse_desc, extra_atoms, owner_slots):
    env_rows, _ = env_desc.shape
    width = sparse_desc.shape[0] * Y * XL
    other_desc = move(env_desc, other_core)
    half = sparse_unit(sparse_desc)
    from_up, from_down = move(half, up), move(half, down)
    near = move(half, across)
    *members, inverse, more_owner, pick, pick_more = book(extra_atoms, owner_slots, env_rows)
    envs = env_unit(env_desc, other_desc, (near, inverse))
    sums = jax.ShapeDtypeStruct((HELD_ROWS, 2 * LANES), jnp.float32)
    sums_0 = call(early_call, (), (half, near), envs, members, sums)
    far = move(choose(from_up, from_down, (sums_0,)), onward)
    near_up = move(from_up, across)
    sums_1 = call(early_call, (), (from_up, from_down), envs, members, sums)
    after = (sums_1,)
    count = half.shape[0]
    near_down = move(rows_of(from_down, 0, count, after), across)
    by_y = count // 16 * 3 // 8 * 16
    near_far_a = move(rows_of(near, 0, by_y, (far, *after)), opposite)
    near_far_b = move(rows_of(far, by_y, count - by_y, after), across)
    sums_2 = call(early_call, (), (near_up, far), envs, members, sums)
    codes = call(
        last_call,
        (sums_0, sums_1, sums_2, inverse, more_owner),
        (near_down, near_far_a, near_far_b),
        envs,
        members,
        jax.ShapeDtypeStruct((ROWS // 2, 2 * SENT, LANES), jnp.int16),
    )
    got = lax.all_to_all(codes.reshape(ROWS, SENT, LANES), "rows", 0, 0, tiled=True)
    return combine(got.reshape(CHIPS, CORE * SENT, LANES), pick, pick_more, width)


def solution(mesh):
    placed = (P(("sparse", "rows"), None), P("sparse", None), P("sparse", None), P("sparse", None))
    return jax.shard_map(
        on_device,
        mesh=mesh,
        in_specs=placed,
        out_specs=P(("sparse", "rows"), None),
        check_vma=False,
    )
```

```python
import functools

import jax
import jax.numpy as jnp
from jax import lax
from jax.experimental import pallas as pl
from jax.experimental.pallas import tpu as pltpu
from jax.sharding import PartitionSpec as P

Y, XL, Z, XH, CORE = 4, 2, 8, 2, 2
CHIPS = Z * XH
ROWS = CHIPS * CORE
KEEP = 4
HELD = ROWS * KEEP
HELD_ROWS = HELD + 8
SENT = 8 * KEEP + 8
LANES = 128
MIB = 1 << 20
SHIFTS = ((0, 0), (0, 1), (3, 0), (1, 0), (3, 1), (2, 0), (1, 1), (2, 1))
STEPS, LEAST, ZERO = 512.0, 126.0, 32768

VMEM = pl.BlockSpec(memory_space=pltpu.VMEM)
ANY = pl.BlockSpec(memory_space=pl.ANY)


def place(y, xl, z, xh, core):
    return (((y % Y * XL + xl) * Z + z % Z) * XH + xh) * CORE + core


def move(array, to):
    pairs = []
    for y in range(Y):
        for xl in range(XL):
            for z in range(Z):
                for xh in range(XH):
                    for core in range(CORE):
                        target = to(y, xl, z, xh, core)
                        if target is not None:
                            pairs.append((place(y, xl, z, xh, core), place(*target)))
    return lax.ppermute(array, ("sparse", "rows"), pairs)


def across(y, xl, z, xh, core):
    return y, 1 - xl, z, (xh + core) % XH, core


def onward(y, xl, z, xh, core):
    return (y + 1 if core == 0 else y - 1), xl, z, xh, core


def opposite(y, xl, z, xh, core):
    return y + 2, xl, z, xh, core


def back(y, xl, z, xh, core):
    return (y - 1 if core == 0 else y + 1), xl, z, xh, core


def other_core(y, xl, z, xh, core):
    return y, xl, z, xh, 1 - core


def unit(desc):
    values = desc.astype(jnp.float32)
    scale = 1.0 / jnp.sqrt(jnp.sum(values * values, axis=1, keepdims=True) + 1e-06)
    return (values * scale).astype(jnp.bfloat16)


def in_hbm(array):
    return pltpu.with_memory_space_constraint(array, pltpu.HBM)


def in_vmem(array):
    return pltpu.with_memory_space_constraint(array, pltpu.VMEM)


def params(mib):
    return pltpu.CompilerParams(vmem_limit_bytes=mib * MIB)


def cost(flops, moved):
    return pl.CostEstimate(flops=flops, bytes_accessed=moved, transcendentals=0)


def sparse_kernel(desc_ref, half_ref, raw, sem):
    half = half_ref.shape[0]
    at = pl.multiple_of(lax.axis_index("rows") % CORE * half, half)
    copy = pltpu.make_async_copy(desc_ref.at[pl.ds(at, half)], raw, sem)
    copy.start()
    copy.wait()
    half_ref[...] = unit(raw[...])


def sparse_unit(desc):
    rows, width = desc.shape
    half = rows // CORE
    return pl.pallas_call(
        sparse_kernel,
        in_specs=[ANY],
        out_specs=VMEM,
        out_shape=jax.ShapeDtypeStruct((half, width), jnp.bfloat16),
        scratch_shapes=[pltpu.VMEM((half, width), jnp.bfloat16), pltpu.SemaphoreType.DMA],
        compiler_params=params(8),
        cost_estimate=cost(4 * half * width, 4 * half * width),
        name="sparse_unit",
    )(in_hbm(desc))


def env_kernel(own_desc, other_desc, *refs):
    own_ref, other_ref, raw, sems = refs[-4:]
    rows = own_desc.shape[0]
    tiles = sems.shape[0] // 2
    tile = rows // tiles
    steps = []
    for env, (desc, out) in enumerate(((own_desc, own_ref), (other_desc, other_ref))):
        for i in range(tiles):
            copy = pltpu.make_async_copy(
                desc.at[pl.ds(i * tile, tile)],
                raw.at[env, pl.ds(i * tile, tile)],
                sems.at[env * tiles + i],
            )
            steps.append((copy, env, out, slice(i * tile, (i + 1) * tile)))
    for copy, *_ in steps:
        copy.start()
    for copy, env, out, to in steps:
        copy.wait()
        out[to] = unit(raw[env, to])


def env_unit(own, other, after):
    rows, width = own.shape
    whole = jax.ShapeDtypeStruct((rows, width), jnp.bfloat16)
    return pl.pallas_call(
        env_kernel,
        in_specs=[ANY] * (2 + len(after)),
        out_specs=[VMEM] * 2,
        out_shape=[whole, whole],
        scratch_shapes=[
            pltpu.VMEM((CORE, rows, width), jnp.bfloat16),
            pltpu.SemaphoreType.DMA((8,)),
        ],
        compiler_params=params(24),
        cost_estimate=cost(16 * rows * width, 8 * rows * width),
        name="env_unit",
    )(in_hbm(own), other, *after)


def rows_kernel(array_ref, *refs, begin):
    refs[-1][...] = array_ref[begin : begin + refs[-1].shape[0]]


def rows_of(array, begin, count, after):
    width = array.shape[1]
    return pl.pallas_call(
        functools.partial(rows_kernel, begin=begin),
        in_specs=[VMEM] + [ANY] * len(after),
        out_specs=VMEM,
        out_shape=jax.ShapeDtypeStruct((count, width), array.dtype),
        compiler_params=params(4),
        cost_estimate=cost(0, 4 * count * width),
        name="rows_of",
    )(array, *after)


def book_kernel(
    extra_ref,
    slots_ref,
    own_ref,
    other_ref,
    inverse_ref,
    more_owner_ref,
    pick_ref,
    pick_more_ref,
    *,
    env_rows,
):
    groups = extra_ref.shape[1]
    parts = groups // LANES
    atom_min = env_rows // (2 * (groups // ROWS))
    chip_rows = CORE * env_rows
    my_row = lax.axis_index("rows")
    core = my_row % CORE
    chip = my_row // CORE
    base = chip * chip_rows

    def rows_of(ref):
        return jnp.concatenate([ref[:, i * LANES : (i + 1) * LANES] for i in range(parts)], axis=0)

    atoms = rows_of(extra_ref) + (atom_min - 1)
    slots = rows_of(slots_ref)
    lane_i = lax.broadcasted_iota(jnp.int32, (LANES, LANES), 0)
    lane_j = lax.broadcasted_iota(jnp.int32, (LANES, LANES), 1)
    upto = (lane_i <= lane_j).astype(jnp.float32)
    along = jnp.dot(
        atoms.astype(jnp.float32).astype(jnp.bfloat16),
        upto.astype(jnp.bfloat16),
        preferred_element_type=jnp.float32,
    )
    rows_total = along[:, LANES - 1 :].astype(jnp.int32)
    ends = along.astype(jnp.int32)
    part = lax.broadcasted_iota(jnp.int32, (parts, LANES), 0)
    for i in range(parts - 1):
        ends = ends + jnp.where(part > i, rows_total[i : i + 1, :], 0)
    starts = ends - atoms

    found = (ends <= base).astype(jnp.int32)
    first = jnp.sum(jnp.sum(found, axis=0, keepdims=True), axis=1, keepdims=True)

    row = lax.broadcasted_iota(jnp.int32, (HELD_ROWS, 1), 0)
    held = first + ((row // KEEP - first) & (ROWS - 1)) + ROWS * (row % KEEP)
    held = jnp.where(row < HELD, held, jnp.where(row == HELD, first + HELD, -1))
    more_owner_ref[...] = jnp.broadcast_to((first + HELD) & (ROWS - 1), more_owner_ref.shape)
    lane = lax.broadcasted_iota(jnp.int32, (HELD_ROWS, LANES), 1)
    found_start = jnp.zeros((HELD_ROWS, LANES), jnp.int32)
    found_end = jnp.zeros((HELD_ROWS, LANES), jnp.int32)
    for i in range(parts):
        here = held == lane + i * LANES
        found_start = jnp.where(here, starts[i : i + 1, :], found_start)
        found_end = jnp.where(here, ends[i : i + 1, :], found_end)
    start = jnp.sum(found_start, axis=1, keepdims=True)
    end = jnp.sum(found_end, axis=1, keepdims=True)
    inverse_ref[...] = 1.0 / jnp.maximum(end - start, 1).astype(jnp.float32)
    lower = jnp.maximum(start, base)

    def member(begin, count):
        position = begin + lax.broadcasted_iota(jnp.int32, (HELD_ROWS, count), 1)
        inside = (position >= lower) & (position < end)
        return inside.astype(jnp.float32).astype(jnp.bfloat16)

    own_ref[...] = member(base + core * env_rows, env_rows)
    other_ref[...] = member(base + (1 - core) * env_rows, env_rows)

    ends_down = ends.astype(jnp.float32).T.astype(jnp.int32)
    slots_down = slots.astype(jnp.float32).T.astype(jnp.int32)
    from_lane = lax.broadcasted_iota(jnp.int32, (1, LANES), 1)
    limit = (from_lane // (2 * KEEP)) * chip_rows
    ended = jnp.zeros((LANES, LANES), jnp.int32)
    for i in range(parts):
        ended = ended + (ends_down[:, i : i + 1] <= limit).astype(jnp.int32)
    firsts = jnp.sum(ended, axis=0, keepdims=True)
    sent = firsts + ((my_row - firsts) & (ROWS - 1)) + ROWS * (from_lane % KEEP)
    below = lax.broadcasted_iota(jnp.int32, (LANES, LANES), 0)
    more = firsts + HELD

    def slot_of(structure):
        found = jnp.zeros((LANES, LANES), jnp.int32)
        for i in range(parts):
            found = jnp.where(structure == below + i * LANES, slots_down[:, i : i + 1] + 1, found)
        return jnp.sum(found, axis=0, keepdims=True) - 1

    def picks(ref, slot, part):
        count = groups // ROWS
        target = lax.broadcasted_iota(jnp.int32, ref.shape, 0)
        chosen = (target % count == slot) & (target // count == part)
        ref[...] = chosen.astype(jnp.float32).astype(jnp.bfloat16)

    picks(pick_ref, slot_of(sent), (from_lane // KEEP) % 2)
    more_slot = jnp.where((more & (ROWS - 1)) == my_row, slot_of(more), -1)
    picks(pick_more_ref, more_slot, from_lane % 8)


def book(extra_atoms, owner_slots, env_rows):
    str_dev = extra_atoms.shape[1] // ROWS

    return pl.pallas_call(
        functools.partial(book_kernel, env_rows=env_rows),
        in_specs=[VMEM, VMEM],
        out_specs=[VMEM] * 6,
        out_shape=[
            jax.ShapeDtypeStruct((HELD_ROWS, env_rows), jnp.bfloat16),
            jax.ShapeDtypeStruct((HELD_ROWS, env_rows), jnp.bfloat16),
            jax.ShapeDtypeStruct((HELD_ROWS, 1), jnp.float32),
            jax.ShapeDtypeStruct((1, LANES), jnp.int32),
            jax.ShapeDtypeStruct((2 * str_dev, LANES), jnp.bfloat16),
            jax.ShapeDtypeStruct((8 * str_dev, LANES), jnp.bfloat16),
        ],
        compiler_params=params(8),
        cost_estimate=cost(1 << 22, 1 << 20),
        name="book",
    )(extra_atoms, owner_slots)


def power_parts(env, block):
    inner = lax.dot_general(env, block, (((1,), (1,)), ((), ())), preferred_element_type=jnp.float32)
    square = inner * inner
    kernel = square * square
    high = kernel.astype(jnp.bfloat16)
    return high, (kernel - high.astype(jnp.float32)).astype(jnp.bfloat16)


def block_sums(*refs):
    *pieces, own, other, of_own, of_other, block, high, low = refs
    at = 0
    for piece in pieces:
        block[at : at + piece.shape[0]] = piece[...]
        at += piece.shape[0]
    rows = own.shape[0]
    tile = 512
    for begin, env in ((0, own), (rows, other)):
        for i in range(0, rows, tile):
            to = slice(begin + i, begin + i + tile)
            high[to], low[to] = power_parts(env[i : i + tile], block[...])

    def dot(member, part):
        return jnp.dot(member[...], part, preferred_element_type=jnp.float32)

    return (
        dot(of_own, high[:rows])
        + dot(of_own, low[:rows])
        + dot(of_other, high[rows:])
        + dot(of_other, low[rows:])
    )


def early_call(a, b, own, other, of_own, of_other, out, block, high, low):
    out[...] = block_sums(a, b, own, other, of_own, of_other, block, high, low)


def encode(sums):
    position = (jnp.log2(jnp.maximum(sums, 2.0**-126)) + LEAST) * STEPS
    code = jnp.clip(jnp.round(position), 0.0, 65534.0).astype(jnp.int32) + (1 - ZERO)
    return jnp.where(sums >= 2.0**-126, code, -ZERO)


def decode(codes):
    code = codes.astype(jnp.int32) + (ZERO - 1)
    return jnp.where(code < 0, 0.0, jnp.exp2(code.astype(jnp.float32) * (1.0 / STEPS) - LEAST))


def last_call(sums_0, sums_1, sums_2, inverse, more_owner, *refs):
    *operands, out_ref, block, high, low = refs
    last = block_sums(*operands, block, high, low)
    means = [part * inverse[...] for part in (sums_0[...], sums_1[...], sums_2[...], last)]
    tiles = (ROWS // 2, 2 * KEEP, LANES)
    lower = lax.broadcasted_iota(jnp.int32, tiles, 1) < KEEP
    owner = 2 * lax.broadcasted_iota(jnp.int32, tiles, 0)
    packed = ([], [])
    more = []
    for mean in means:
        both = encode(mean[:HELD]).reshape(ROWS // 2, 2 * KEEP, 2 * LANES)
        left, right = both[:, :, :LANES], both[:, :, LANES:]
        packed[0].append(jnp.where(lower, left, jnp.roll(right, KEEP, axis=1)))
        packed[1].append(jnp.where(lower, jnp.roll(left, KEEP, axis=1), right))
        more += [mean[HELD : HELD + 1, :LANES], mean[HELD : HELD + 1, LANES:]]
    codes = encode(jnp.concatenate(more, axis=0)).reshape(1, 8, LANES)
    for i in range(2):
        here = owner + i == more_owner[...].reshape(1, 1, LANES)
        packed[i].append(jnp.where(here, codes, -ZERO))
    rows = packed[0] + packed[1]
    for i in range(0, len(rows), 2):
        both = jnp.concatenate(rows[i : i + 2], axis=1)
        out_ref[:, 8 * i : 8 * i + 16] = both.astype(jnp.int16)


def call(kernel, first, pieces, envs, members, out_shape):
    own, other = envs
    rows, width = own.shape
    columns = 2 * LANES
    operands = (*first, *pieces, in_vmem(own), in_vmem(other), *members)
    return pl.pallas_call(
        kernel,
        in_specs=[VMEM] * len(operands),
        out_specs=VMEM,
        out_shape=out_shape,
        scratch_shapes=[
            pltpu.VMEM((columns, width), jnp.bfloat16),
            pltpu.VMEM((2 * rows, columns), jnp.bfloat16),
            pltpu.VMEM((2 * rows, columns), jnp.bfloat16),
        ],
        compiler_params=params(16),
        cost_estimate=cost(4 * rows * width * columns, 4 * rows * width),
        name=kernel.__name__,
    )(*operands)


def combine_kernel(got_ref, pick_ref, pick_more_ref, out_ref):
    block = lax.axis_index("sparse")
    y, xl = block // XL, block % XL
    count = out_ref.shape[0]
    tiles = []
    for i in range(CORE * SENT // 16):
        values = decode(got_ref[:, 16 * i : 16 * (i + 1), :])
        for j in range(2):
            tiles.append(values[:, 8 * j : 8 * (j + 1), :].reshape(8 * CHIPS, LANES))

    def picked(pick, tile):
        high = tile.astype(jnp.bfloat16)
        low = (tile - high.astype(jnp.float32)).astype(jnp.bfloat16)
        return jnp.dot(pick, high, preferred_element_type=jnp.float32) + jnp.dot(
            pick, low, preferred_element_type=jnp.float32
        )

    for core in range(CORE):
        *held, more = tiles[core * SENT // 8 : (core + 1) * SENT // 8]
        more = picked(pick_more_ref[...], more)
        for i, tile in enumerate(held):
            sums = picked(pick_ref[...], tile) + more[2 * i * count : 2 * (i + 1) * count]
            for half in range(2):
                dy, dx = SHIFTS[2 * i + half]
                dy = dy if core == 0 else Y - dy
                column = ((y + dy) % Y * XL + (xl + dx) % XL) * CORE + core
                at = pl.multiple_of(column * LANES, LANES)
                out_ref[:, pl.ds(at, LANES)] = sums[half * count : (half + 1) * count]


def combine(got, pick, pick_more, width):
    return pl.pallas_call(
        combine_kernel,
        in_specs=[VMEM, VMEM, VMEM],
        out_specs=VMEM,
        out_shape=jax.ShapeDtypeStruct((pick.shape[0] // 2, width), jnp.float32),
        compiler_params=params(8),
        name="combine",
    )(got, pick, pick_more)


def on_device(env_desc, sparse_desc, extra_atoms, owner_slots):
    env_rows, _ = env_desc.shape
    width = sparse_desc.shape[0] * Y * XL
    other_desc = move(env_desc, other_core)
    half = sparse_unit(sparse_desc)
    count = half.shape[0]
    first = move(half, onward)
    near = move(half, across)
    second = move(rows_of(half, 0, count, (other_desc,)), back)
    far = move(first, onward)
    near_first, near_second = move(first, across), move(second, across)
    *members, inverse, more_owner, pick, pick_more = book(extra_atoms, owner_slots, env_rows)
    envs = env_unit(env_desc, other_desc, (near, inverse))
    sums = jax.ShapeDtypeStruct((HELD_ROWS, 2 * LANES), jnp.float32)
    sums_0 = call(early_call, (), (half, near), envs, members, sums)
    sums_1 = call(early_call, (), (first, second), envs, members, sums)
    by_y = count // 16 * 3 // 8 * 16
    near_far_a = move(rows_of(near, 0, by_y, (far, sums_1)), opposite)
    near_far_b = move(rows_of(far, by_y, count - by_y, (sums_1,)), across)
    sums_2 = call(early_call, (), (near_first, far), envs, members, sums)
    codes = call(
        last_call,
        (sums_0, sums_1, sums_2, inverse, more_owner),
        (near_second, near_far_a, near_far_b),
        envs,
        members,
        jax.ShapeDtypeStruct((ROWS // 2, 2 * SENT, LANES), jnp.int16),
    )
    got = lax.all_to_all(codes.reshape(ROWS, SENT, LANES), "rows", 0, 0, tiled=True)
    return combine(got.reshape(CHIPS, CORE * SENT, LANES), pick, pick_more, width)


def solution(mesh):
    placed = (P(("sparse", "rows"), None), P("sparse", None), P("sparse", None), P("sparse", None))
    return jax.shard_map(
        on_device,
        mesh=mesh,
        in_specs=placed,
        out_specs=P(("sparse", "rows"), None),
        check_vma=False,
    )
```
